32 devices in a mesh: parts: 2 (over x), slab: 16 (over z, y, core).
Axes of the slice: x: 2, y: 2, z: 4, core: 2. Of those that a mesh axis runs over, the one named last changes fastest.
Arguments:
- e_field: float32 [3, 512, 64, 128], P(None, ('parts', 'slab')), parts along dimension 1, may hold values from -6 to 6
- h_field: float32 [3, 512, 64, 128], P(None, ('parts', 'slab')), parts along dimension 1, may hold values from -6 to 6
- phasor_re: float32 [3, 512, 64, 128], P(None, ('parts', 'slab')), parts along dimension 1, may hold values from -12 to 12
- phasor_im: float32 [3, 512, 64, 128], P(None, ('parts', 'slab')), parts along dimension 1, may hold values from -12 to 12
- tissue: int32 [512, 64, 128], P(('parts', 'slab')), parts along dimension 0, may hold values from 0 to 77, as said below
- sigma_table: float32 [77], replicated, may hold values from 0.004 to 0.25
- eps_table: float32 [77], replicated, may hold values from 5 to 80
- density_table: float32 [77], replicated, may hold values from 0.9 to 1.9
- brick_anchor: int32 [3, 5120], P(None, ('parts', 'slab')), parts along dimension 1, may hold values from 0 to 120, as said below
- brick_helper: int32 [5120], P(('parts', 'slab')), parts along dimension 0, may hold values from 0 to 15, as said below
- brick_count: int32 [32], P(('parts', 'slab')), parts along dimension 0, may hold values from 16 to 160, as said below
Outputs:
- e_final: float32 [3, 512, 64, 128], P(None, ('parts', 'slab')), parts along dimension 1
- h_final: float32 [3, 512, 64, 128], P(None, ('parts', 'slab')), parts along dimension 1
- sar_table: float32 [5120, 512], P(('parts', 'slab')), parts along dimension 0
The draws below stay inside these ranges and needn't reach their ends.
There are 2 independent parts, one for each index of `parts`. The reference program is written for one: setup_inputs(seed, part) draws one part's arguments, and reference() takes and returns one part's arrays. A program takes and returns all parts, laid end to end along the dimension named above; an argument that names none is the same for every part. Nothing has to cross between parts.
Inputs may be any that keep to these rules, and one draw needn't show every extreme that they name: 0 marks air; tissue k > 0 takes entry k - 1 of each table. `brick_count`: every device lists 10 + 6 or more bricks; some device lists 160. `brick_helper`: among the 160 entries of one device no helper appears more than 10 times; in every draw some helper receives 10 listed bricks from every device. `brick_anchor`: row 0 lies in 0 to 8, row 1 in 0 to 56, row 2 in 0 to 120: every brick lies inside its owner's block.
All inputs are finite; a program needn't handle non-finite values.
Results may differ from the reference program's by a relative error of at most 0.00016.
Values sent between devices are 32-bit elements; how exact they have to be, the bound alone decides.
A program may use at most 64 MiB of HBM per device.

```python
import math
import jax
import jax.numpy as jnp
from jax import lax

CX = 16
NY = 64
NZ = 128
NTIS = 77
STEPS = 6
APRON = 10
BRICK = 8
MAXC = 160
PERIOD = 2600
START = 325
CAP = 10
NX = 256
N_SLAB = 16


def draw_tissue(key, part):
    key = jax.random.fold_in(key, 11)
    label_key, size_key, pocket_key = jax.random.split(key, 3)
    labels = jax.random.randint(label_key, (NX, NY, NZ), 1, NTIS + 1)
    percent = jax.random.randint(size_key, (NX, 1, 1), 70, 96)
    across_y = ((2 * jnp.arange(NY, dtype=jnp.int32) + 1 - NY) * NZ // 8)[None, :, None]
    across_z = ((2 * jnp.arange(NZ, dtype=jnp.int32) + 1 - NZ) * NY // 8)[None, None, :]
    reach = NY * NZ * percent // 800
    inside = across_y * across_y + across_z * across_z <= reach * reach
    pocket = jax.random.randint(pocket_key, (NX, NY, NZ), 0, 6) == 0
    return jnp.where(inside & jnp.logical_not(pocket), labels, 0).astype(jnp.int32)


def draw_brick_count(key, part):
    key = jax.random.fold_in(key, 23)
    level_key, top_key = jax.random.split(key)
    slabs = NX // CX
    levels = jax.random.randint(level_key, (slabs,), 0, 64)
    top = jax.random.randint(top_key, (), 0, slabs)
    levels = jnp.where(jnp.arange(slabs) == top, 63, levels)
    lowest = CAP + 6
    return (lowest + (MAXC - lowest) * levels * levels // 3969).astype(jnp.int32)


def draw_brick_helper(key, part):
    key = jax.random.fold_in(key, 37)
    slabs = NX // CX
    star_key, order_key = jax.random.split(key)
    star = jax.random.randint(star_key, (), 0, slabs)

    def one_device(device_key):
        first_key, second_key = jax.random.split(device_key)
        order = jax.random.permutation(first_key, CAP * (slabs - 1))[:MAXC - CAP] // CAP
        order = order + (order >= star).astype(order.dtype)
        entries = jnp.concatenate([jnp.full((CAP,), star, jnp.int32), order.astype(jnp.int32)])
        leading = CAP + 6
        mixed = jax.random.permutation(second_key, leading)
        return jnp.concatenate([entries[:leading][mixed], entries[leading:]])
    table = jax.vmap(one_device)(jax.random.split(order_key, slabs))
    return table.reshape(-1).astype(jnp.int32)


def draw_brick_anchor(key, part):
    key = jax.random.fold_in(key, 53)
    slabs = NX // CX
    first_key, second_key, third_key = jax.random.split(key, 3)
    total = slabs * MAXC
    along_x = jax.random.randint(first_key, (total,), 0, CX - BRICK + 1)
    along_y = jax.random.randint(second_key, (total,), 0, NY - BRICK + 1)
    along_z = jax.random.randint(third_key, (total,), 0, NZ - BRICK + 1)
    return jnp.stack([along_x, along_y, along_z]).astype(jnp.int32)


def level_of(own_key, extent, pieces, low, largest):
    gain = 1.0
    for position, blocks in pieces:
        steps = jax.random.uniform(jax.random.fold_in(jax.random.fold_in(own_key, 6), position), (blocks,), jnp.float32, low / len(pieces), largest / len(pieces))
        gain = gain * jnp.repeat(jnp.exp(steps), extent[position] // blocks).reshape((-1,) + (1,) * (len(extent) - 1 - position))
    return gain


def centred(key, dims, deviation, bound, cuts=(), held_as=jnp.bfloat16):
    result = jax.random.normal(key, dims, jnp.float32) * deviation
    if len(cuts) > 0:
        result = level_of(key, dims, cuts, -0.22, 0.18) * result
    return jnp.clip(result, min=-bound, max=bound).astype(held_as)


def setup_inputs(seed: int = 0, part: int = 0) -> dict:
    key_list = jax.random.split(jax.random.key(seed), 12)
    part_splits = jax.random.split(jax.random.fold_in(key_list[11], part), 12)
    return {
        "e_field": centred(part_splits[0], (3, NX, NY, NZ), 1.0, 6.0, ((1, 16),), jnp.float32),
        "h_field": centred(part_splits[1], (3, NX, NY, NZ), 1.0, 6.0, ((1, 16),), jnp.float32),
        "phasor_re": centred(part_splits[2], (3, NX, NY, NZ), 2.0, 12.0, ((1, 16),), jnp.float32),
        "phasor_im": centred(part_splits[3], (3, NX, NY, NZ), 2.0, 12.0, ((1, 16),), jnp.float32),
        "tissue": draw_tissue(jax.random.fold_in(jax.random.fold_in(key_list[11], part), 71), part),
        "sigma_table": jnp.clip(jnp.exp(jax.random.uniform(key_list[5], (NTIS,), jnp.float32, math.log(0.004), math.log(0.25))), 0.004, 0.25),
        "eps_table": jnp.clip(jnp.exp(jax.random.uniform(key_list[6], (NTIS,), jnp.float32, math.log(5.0), math.log(80.0))), 5.0, 80.0),
        "density_table": jnp.clip(jax.random.uniform(key_list[7], (NTIS,), jnp.float32, 0.9, 1.9), 0.9, 1.9),
        "brick_anchor": draw_brick_anchor(jax.random.fold_in(jax.random.fold_in(key_list[11], part), 71), part),
        "brick_helper": draw_brick_helper(jax.random.fold_in(jax.random.fold_in(key_list[11], part), 71), part),
        "brick_count": draw_brick_count(jax.random.fold_in(jax.random.fold_in(key_list[11], part), 71), part),
    }


COURANT = 0.5
FLOOR_SHARE = 0.2


def forward_diff(values, axis):
    tail_zero = jnp.zeros_like(lax.slice_in_dim(values, 0, 1, axis=axis))
    moved = jnp.concatenate([lax.slice_in_dim(values, 1, values.shape[axis], axis=axis), tail_zero], axis)
    return moved - values


def backward_diff(values, axis):
    head_zero = jnp.zeros_like(lax.slice_in_dim(values, 0, 1, axis=axis))
    moved = jnp.concatenate([head_zero, lax.slice_in_dim(values, 0, values.shape[axis] - 1, axis=axis)], axis)
    return values - moved


def window_sum(values, axis):
    window_shape = [1, 1, 1]
    window_shape[axis] = 2 * APRON + 1
    padding_pairs = [(0, 0), (0, 0), (0, 0)]
    padding_pairs[axis] = (APRON, APRON)
    return lax.reduce_window(values, jnp.zeros((), values.dtype), lax.add, tuple(window_shape), (1, 1, 1), tuple(padding_pairs))


def reference(e_field, h_field, phasor_re, phasor_im, tissue, sigma_table, eps_table, density_table, brick_anchor, brick_helper, brick_count):
    inside = tissue > 0
    table_rows = jnp.clip(tissue - 1, 0, NTIS - 1)
    conductivity = jnp.where(inside, sigma_table[table_rows], 0.0)
    eps_rel = 1.0 + jnp.where(inside, (eps_table - 1.0)[table_rows], 0.0)
    density = jnp.where(inside, density_table[table_rows], 0.0)
    damping = conductivity / (2.0 * eps_rel)
    coef_keep = (1.0 - damping) / (1.0 + damping)
    coef_curl = COURANT / (eps_rel * (1.0 + damping))
    ele_x, ele_y, ele_z = e_field[0], e_field[1], e_field[2]
    mag_x, mag_y, mag_z = h_field[0], h_field[1], h_field[2]
    re_total, im_total = phasor_re, phasor_im
    for step in range(STEPS):
        mag_x = mag_x - COURANT * (forward_diff(ele_z, 1) - forward_diff(ele_y, 2))
        mag_y = mag_y - COURANT * (forward_diff(ele_x, 2) - forward_diff(ele_z, 0))
        mag_z = mag_z - COURANT * (forward_diff(ele_y, 0) - forward_diff(ele_x, 1))
        ele_x = coef_keep * ele_x + coef_curl * (backward_diff(mag_z, 1) - backward_diff(mag_y, 2))
        ele_y = coef_keep * ele_y + coef_curl * (backward_diff(mag_x, 2) - backward_diff(mag_z, 0))
        ele_z = coef_keep * ele_z + coef_curl * (backward_diff(mag_y, 0) - backward_diff(mag_x, 1))
        phase_angle = 2.0 * math.pi * (START + step + 1) / PERIOD
        electric = jnp.stack([ele_x, ele_y, ele_z])
        re_total = re_total + math.cos(phase_angle) * electric
        im_total = im_total - math.sin(phase_angle) * electric
    heating = 0.5 * conductivity * jnp.sum(re_total * re_total + im_total * im_total, axis=0)
    q_cube = window_sum(window_sum(window_sum(heating, 2), 1), 0)
    m_cube = window_sum(window_sum(window_sum(density, 2), 1), 0)
    sar_avg = q_cube / jnp.maximum(m_cube, FLOOR_SHARE * (2 * APRON + 1) ** 3)
    helpers = brick_helper.reshape(N_SLAB, MAXC).astype(jnp.int32)
    slot_index = jnp.arange(MAXC, dtype=jnp.int32)
    live_slots = slot_index[None, :] < brick_count.astype(jnp.int32)[:, None]
    earlier = (helpers[:, :, None] == helpers[:, None, :]) & (slot_index[None, None, :] < slot_index[None, :, None])
    slot_rank = jnp.sum(earlier.astype(jnp.int32), axis=2)
    owners = jnp.arange(N_SLAB, dtype=jnp.int32)[:, None]
    target = helpers * (N_SLAB * CAP) + owners * CAP + slot_rank
    target = jnp.where(live_slots, target, N_SLAB * N_SLAB * CAP).reshape(-1).astype(jnp.int32)
    corner_x = (owners * CX + brick_anchor[0].reshape(N_SLAB, MAXC)).reshape(-1).astype(jnp.int32)

    def cut_brick(start_x, start_y, start_z):
        return lax.dynamic_slice(sar_avg, (start_x, start_y, start_z), (BRICK, BRICK, BRICK)).reshape(-1)

    brick_cores = jax.vmap(cut_brick)(corner_x, brick_anchor[1].astype(jnp.int32), brick_anchor[2].astype(jnp.int32))
    sar_table = jnp.zeros((N_SLAB * N_SLAB * CAP, BRICK ** 3), sar_avg.dtype).at[target].set(brick_cores, mode="drop")
    return (jnp.stack([ele_x, ele_y, ele_z]), jnp.stack([mag_x, mag_y, mag_z]), sar_table)
```

```python
import functools
import math

import jax
import jax.numpy as jnp
import numpy as np
from jax import lax
from jax.experimental import pallas as pl
from jax.experimental.pallas import tpu as pltpu
from jax.sharding import PartitionSpec as P

STEPS = 6
APRON = 10
BRICK = 8
PERIOD = 2600
START = 325
COURANT = 0.5
FLOOR_SHARE = 0.2
PAD = 8
LANES = 128
F32 = jnp.float32
VMEM_SPEC = pl.BlockSpec(memory_space=pltpu.VMEM)
SMEM_SPEC = pl.BlockSpec(memory_space=pltpu.SMEM)
ANY_SPEC = pl.BlockSpec(memory_space=pl.ANY)
VMEM_LIMIT = 48 * 1024 * 1024


def band(across_z):
    row = lax.broadcasted_iota(jnp.int32, (across_z, across_z), 0)
    col = lax.broadcasted_iota(jnp.int32, (across_z, across_z), 1)
    return (jnp.abs(row - col) <= APRON).astype(F32)


def along_z(rows, matrix):
    return jnp.dot(rows, matrix, precision=lax.Precision.HIGHEST, preferred_element_type=F32)


def clear_margins(padded):
    layers, rows, lanes = padded.shape
    zero = jnp.zeros((layers, 16, lanes), F32)
    padded[:, 0:16] = zero
    padded[:, rows - 16 : rows] = zero


def along_y(padded, triples, layer, across_y):
    count = across_y + 24
    triples[layer, 0:count] = (
        padded[layer, 0:count] + padded[layer, 1 : count + 1] + padded[layer, 2 : count + 2]
    )
    total = triples[layer, 6 : 6 + across_y]
    for part in range(1, 7):
        total = total + triples[layer, 6 + 3 * part : 6 + 3 * part + across_y]
    return total


def window_21(layers, count):
    two = [a + b for a, b in zip(layers[:-1], layers[1:])]
    four = [a + b for a, b in zip(two[:-2], two[2:])]
    eight = [a + b for a, b in zip(four[:-4], four[4:])]
    return [
        (eight[i] + eight[i + 8]) + (four[i + 16] + layers[i + 20]) for i in range(count)
    ]


def material_kernel(tables, tissue, keep, curl, sigma, mass, padded, triples):
    width, across_y, across_z = tissue.shape
    shape = (8, LANES)
    sig = jnp.broadcast_to(tables[0:1, :], shape)
    eps = 1.0 + jnp.broadcast_to(tables[1:2, :], shape)
    rho = jnp.broadcast_to(tables[2:3, :], shape)
    damping = sig / (2.0 * eps)
    keep_row = (1.0 - damping) / (1.0 + damping)
    curl_row = COURANT / (eps * (1.0 + damping))
    clear_margins(padded)
    matrix = band(across_z)

    def one_layer(layer, carry):
        for y in range(0, across_y, 8):
            ids = tissue[layer, y : y + 8, :]
            keep[layer, y : y + 8, :] = jnp.take_along_axis(keep_row, ids, axis=1)
            curl[layer, y : y + 8, :] = jnp.take_along_axis(curl_row, ids, axis=1)
            sigma[layer, y : y + 8, :] = jnp.take_along_axis(sig, ids, axis=1)
            padded[layer, 16 + y : 24 + y, :] = jnp.take_along_axis(rho, ids, axis=1)
        return carry

    lax.fori_loop(0, width, one_layer, 0)

    def sum_z(group, carry):
        layers = pl.ds(group * 4, 4)
        rows = padded[layers, 16 : 16 + across_y, :].reshape(4 * across_y, across_z)
        padded[layers, 16 : 16 + across_y, :] = along_z(rows, matrix).reshape(
            4, across_y, across_z
        )
        return carry

    lax.fori_loop(0, width // 4, sum_z, 0)

    def sum_y(layer, carry):
        mass[layer] = along_y(padded, triples, layer, across_y)
        return carry

    lax.fori_loop(0, width, sum_y, 0)


def field_kernel(
    n,
    phase,
    e_in,
    h_in,
    re_in,
    im_in,
    keep,
    curl,
    sigma,
    mass,
    e_out,
    h_out,
    sar,
    E,
    H,
    re,
    im,
    e_hi,
    e_lo,
    h_lo,
    padded,
    triples,
    heat,
    weight,
    local_sem,
    send_sem,
    hi_sem,
    lo_sem,
    first_sem,
    halo_sem,
):
    width, ny, nz = keep.shape
    last = width - 1
    rows = pl.ds(PAD, ny)
    me = lax.axis_index("slab")
    prev = jnp.maximum(me - 1, 0)
    after = jnp.minimum(me + 1, n - 1)
    has_prev = me > 0
    has_next = me < n - 1

    loads = [
        pltpu.make_async_copy(e_in, E.at[:, :, rows], local_sem.at[0]),
        pltpu.make_async_copy(h_in, H.at[:, :, rows], local_sem.at[1]),
        pltpu.make_async_copy(re_in, re, local_sem.at[2]),
        pltpu.make_async_copy(im_in, im, local_sem.at[3]),
    ]
    for copy in loads:
        copy.start()
    margin = jnp.zeros((3, width, PAD, nz), F32)
    for field in (E, H):
        field[:, :, 0:PAD] = margin
        field[:, :, PAD + ny : 2 * PAD + ny] = margin
    e_hi[...] = jnp.zeros_like(e_hi)
    e_lo[...] = jnp.zeros_like(e_lo)
    h_lo[...] = jnp.zeros_like(h_lo)
    apron = jnp.zeros((APRON, ny, nz), F32)
    for block in (heat, weight):
        block[0:APRON] = apron
        block[APRON + width : 2 * APRON + width] = apron
    clear_margins(padded)

    barrier = pltpu.get_barrier_semaphore()

    @pl.when(has_prev)
    def _():
        pl.semaphore_signal(barrier, inc=1, device_id={"slab": prev})

    @pl.when(has_next)
    def _():
        pl.semaphore_signal(barrier, inc=1, device_id={"slab": after})

    pl.semaphore_wait(barrier, has_prev.astype(jnp.int32) + has_next.astype(jnp.int32))

    def down(slot):
        return pltpu.make_async_remote_copy(
            E.at[pl.ds(1, 2), 0, rows], e_hi.at[slot], send_sem.at[0], hi_sem.at[slot],
            device_id={"slab": prev},
        )

    def up(slot):
        return pltpu.make_async_remote_copy(
            E.at[:, last, rows], e_lo.at[slot, :, pl.ds(0, ny)], send_sem.at[1], lo_sem.at[slot],
            device_id={"slab": after},
        )

    first = pltpu.make_async_remote_copy(
        H.at[pl.ds(1, 2), last, rows], h_lo, first_sem.at[0], first_sem.at[1],
        device_id={"slab": after},
    )

    def halo_down(block, at):
        return pltpu.make_async_remote_copy(
            block.at[pl.ds(APRON, APRON)], block.at[pl.ds(APRON + width, APRON)],
            halo_sem.at[at], halo_sem.at[at + 1], device_id={"slab": prev},
        )

    def halo_up(block, at):
        return pltpu.make_async_remote_copy(
            block.at[pl.ds(width, APRON)], block.at[pl.ds(0, APRON)],
            halo_sem.at[at + 2], halo_sem.at[at + 3], device_id={"slab": after},
        )

    loads[0].wait()
    loads[1].wait()

    @pl.when(has_prev)
    def _():
        down(0).start()

    @pl.when(has_next)
    def _():
        up(0).start()
        first.start()

    weight[APRON : APRON + width] = mass[...]

    @pl.when(has_prev)
    def _():
        halo_down(weight, 4).start()

    @pl.when(has_next)
    def _():
        halo_up(weight, 4).start()

    lane = lax.broadcasted_iota(jnp.int32, (ny, nz), 1)
    not_last = (lane < nz - 1).astype(F32)
    not_first = (lane > 0).astype(F32)

    def z_up(a):
        return pltpu.roll(a, nz - 1, 1) * not_last

    def z_down(a):
        return pltpu.roll(a, 1, 1) * not_first

    def body_of(field, part, layer):
        return field[part, layer, PAD : PAD + ny]

    def y_up(field, part, layer):
        return field[part, layer, PAD + 1 : PAD + 1 + ny]

    def y_down(field, part, layer):
        return field[part, layer, PAD - 1 : PAD - 1 + ny]

    def put(field, part, layer, value):
        field[part, layer, PAD : PAD + ny] = value

    def magnetic(layer, ey_next, ez_next):
        ex, ey, ez = (body_of(E, part, layer) for part in range(3))
        put(H, 0, layer, body_of(H, 0, layer)
            - COURANT * ((y_up(E, 2, layer) - ez) - (z_up(ey) - ey)))
        put(H, 1, layer, body_of(H, 1, layer)
            - COURANT * ((z_up(ex) - ex) - (ez_next - ez)))
        put(H, 2, layer, body_of(H, 2, layer)
            - COURANT * ((ey_next - ey) - (y_up(E, 0, layer) - ex)))

    def magnetic_at(layer):
        magnetic(layer, body_of(E, 1, layer + 1), body_of(E, 2, layer + 1))

    def electric(layer, hy_prev, hz_prev):
        hx, hy, hz = (body_of(H, part, layer) for part in range(3))
        k, c = (keep[layer], curl[layer])
        ex = k * body_of(E, 0, layer) + c * ((hz - y_down(H, 2, layer)) - (hy - z_down(hy)))
        put(E, 0, layer, ex)
        ey = k * body_of(E, 1, layer) + c * ((hx - z_down(hx)) - (hz - hz_prev))
        put(E, 1, layer, ey)
        ez = k * body_of(E, 2, layer) + c * ((hy - hy_prev) - (hx - y_down(H, 0, layer)))
        put(E, 2, layer, ez)

    def electric_at(layer):
        electric(layer, body_of(H, 1, layer - 1), body_of(H, 2, layer - 1))

    def phasor(step, layer):
        for part in range(3):
            value = body_of(E, part, layer)
            re[part, layer] = re[part, layer] + phase[step, 0] * value
            im[part, layer] = im[part, layer] - phase[step, 1] * value

    live = has_prev.astype(F32)

    def one_step(step, carry):
        @pl.when(has_next)
        def _():
            down(step).wait_recv()

        @pl.when(has_prev)
        def _():
            up(step).wait_recv()

        @pl.when(has_prev & (step == 0))
        def _():
            first.wait_recv()

        ex = e_lo[step, 0, 0:ny]
        h_lo[0] = live * (
            h_lo[0]
            - COURANT * ((z_up(ex) - ex) - (body_of(E, 2, 0) - e_lo[step, 2, 0:ny]))
        )
        h_lo[1] = live * (
            h_lo[1]
            - COURANT
            * ((body_of(E, 1, 0) - e_lo[step, 1, 0:ny]) - (e_lo[step, 0, 1 : ny + 1] - ex))
        )
        @pl.when(has_next & (step == 0))
        def _():
            first.wait_send()

        magnetic_at(0)
        magnetic_at(last - 1)
        magnetic(last, e_hi[step, 0], e_hi[step, 1])

        @pl.when(has_prev)
        def _():
            down(step).wait_send()

        @pl.when(has_next)
        def _():
            up(step).wait_send()

        electric(0, h_lo[0], h_lo[1])
        electric_at(last)

        @pl.when(has_prev & (step < STEPS - 1))
        def _():
            down(step + 1).start()

        @pl.when(has_next & (step < STEPS - 1))
        def _():
            up(step + 1).start()

        @pl.when(step == 0)
        def _():
            loads[2].wait()
            loads[3].wait()

        def inner(layer, carry):
            magnetic_at(layer)
            electric_at(layer)
            phasor(step, layer)
            return carry

        lax.fori_loop(1, last - 1, inner, 0)
        electric_at(last - 1)
        phasor(step, last - 1)
        phasor(step, 0)
        phasor(step, last)
        return carry

    lax.fori_loop(0, STEPS, one_step, 0)

    stores = [
        pltpu.make_async_copy(E.at[:, :, rows], e_out, local_sem.at[0]),
        pltpu.make_async_copy(H.at[:, :, rows], h_out, local_sem.at[1]),
    ]
    for copy in stores:
        copy.start()

    matrix = band(nz)

    def heat_z(group, carry):
        layers = pl.ds(group * 4, 4)
        total = jnp.zeros((4, ny, nz), F32)
        for part in range(3):
            real, imag = (re[part, layers], im[part, layers])
            total = total + (real * real + imag * imag)
        total = (0.5 * sigma[layers]) * total
        padded[layers, 16 : 16 + ny, :] = along_z(total.reshape(4 * ny, nz), matrix).reshape(
            4, ny, nz
        )
        return carry

    lax.fori_loop(0, width // 4, heat_z, 0)

    def heat_y(layer, carry):
        heat[APRON + layer] = along_y(padded, triples, layer, ny)
        return carry

    lax.fori_loop(0, width, heat_y, 0)

    @pl.when(has_prev)
    def _():
        halo_down(heat, 0).start()
        halo_down(weight, 4).wait_send()

    @pl.when(has_next)
    def _():
        halo_up(heat, 0).start()
        halo_up(weight, 4).wait_send()
        halo_down(weight, 4).wait_recv()

    @pl.when(has_prev)
    def _():
        halo_up(weight, 4).wait_recv()

    floor_mass = FLOOR_SHARE * (2 * APRON + 1) ** 3

    def weigh(block, carry):
        at = pl.ds(pl.multiple_of(block * 8, 8), 8)
        sums = window_21([weight[i, at] for i in range(width + 2 * APRON)], width)
        for i in range(width):
            sar[i, at] = 1.0 / jnp.maximum(sums[i], floor_mass)
        return carry

    lax.fori_loop(0, ny // 8, weigh, 0)

    @pl.when(has_prev)
    def _():
        halo_down(heat, 0).wait_send()
        halo_up(heat, 0).wait_recv()

    @pl.when(has_next)
    def _():
        halo_up(heat, 0).wait_send()
        halo_down(heat, 0).wait_recv()

    def average(block, carry):
        at = pl.ds(pl.multiple_of(block * 8, 8), 8)
        sums = window_21([heat[i, at] for i in range(width + 2 * APRON)], width)
        for i in range(width):
            sar[i, at] = sums[i] * sar[i, at]
        return carry

    lax.fori_loop(0, ny // 8, average, 0)
    for copy in stores:
        copy.wait()


def brick_kernel(n, codes, sar, table, outgoing, landed, send_sem, recv_sem):
    capacity = outgoing.shape[1]
    me = lax.axis_index("slab")
    barrier = pltpu.get_barrier_semaphore()

    def greet(k, carry):
        pl.semaphore_signal(barrier, inc=1, device_id={"slab": lax.rem(me + k, n)})
        return carry

    lax.fori_loop(1, n, greet, 0)

    shape = (8, LANES)
    lane = lax.broadcasted_iota(jnp.int32, shape, 1)
    sub = lax.broadcasted_iota(jnp.int32, shape, 0)
    even = ((lane - 8 * sub) >= 0) & ((lane - 8 * sub) < 8)
    odd = ((lane - 8 * sub) >= 64) & ((lane - 8 * sub) < 72)

    def one_row(helper, rank):
        code = codes[helper * capacity + rank]
        z = lax.bitwise_and(lax.shift_right_logical(code, 1), 127)
        y = lax.bitwise_and(lax.shift_right_logical(code, 8), 63)
        x = lax.shift_right_logical(code, 14)
        listed = lax.bitwise_and(code, 1).astype(F32)
        from_even = lax.bitwise_and(lane - 8 * sub + z, LANES - 1)
        from_odd = lax.bitwise_and(lane - 8 * sub + (z + 64), LANES - 1)
        for pair in range(BRICK // 2):
            first = jnp.take_along_axis(sar[x + 2 * pair, pl.ds(y, 8), :], from_even, axis=1)
            second = jnp.take_along_axis(sar[x + 2 * pair + 1, pl.ds(y, 8), :], from_odd, axis=1)
            both = jnp.where(even, first, jnp.where(odd, second, 0.0))
            outgoing[helper, pl.ds(rank, 1), pair * LANES : (pair + 1) * LANES] = listed * jnp.sum(
                both, axis=0, keepdims=True
            )

    def fill(helper):
        for rank in range(capacity):
            one_row(helper, rank)

    def copy_to(k):
        helper = lax.rem(me + k, n)
        return pltpu.make_async_remote_copy(
            outgoing.at[helper], landed.at[me], send_sem.at[k], recv_sem.at[me],
            device_id={"slab": helper},
        )

    fill(lax.rem(me + 1, n))
    pl.semaphore_wait(barrier, n - 1)
    copy_to(1).start()

    def send(k, carry):
        fill(lax.rem(me + k, n))
        copy_to(k).start()
        return carry

    lax.fori_loop(2, n, send, 0)
    fill(me)
    landed[me] = outgoing[me]

    def finish(k, carry):
        copy_to(k).wait_send()
        source = lax.rem(me + k, n)
        pltpu.make_async_remote_copy(
            outgoing.at[source], landed.at[source], send_sem.at[k], recv_sem.at[source],
            device_id={"slab": source},
        ).wait_recv()
        return carry

    lax.fori_loop(1, n, finish, 0)
    for source in range(n):
        table[source * capacity : (source + 1) * capacity, :] = landed[source]


def body(
    e_field,
    h_field,
    phasor_re,
    phasor_im,
    tissue,
    sigma_table,
    eps_table,
    density_table,
    brick_anchor,
    brick_helper,
    brick_count,
):
    width, ny, nz = tissue.shape
    n = lax.axis_size("slab")
    grid = jax.ShapeDtypeStruct((width, ny, nz), F32)
    fields = jax.ShapeDtypeStruct(e_field.shape, F32)
    ends = (1, LANES - 1 - sigma_table.shape[0])
    tables = jnp.stack(
        [jnp.pad(sigma_table, ends), jnp.pad(eps_table - 1.0, ends), jnp.pad(density_table, ends)]
    )
    padded = pltpu.VMEM((width, ny + 32, nz), F32)
    params = functools.partial(pltpu.CompilerParams, vmem_limit_bytes=VMEM_LIMIT)

    count_slots = brick_helper.shape[0]
    capacity = max(2, (count_slots + n - 1) // n)
    slot = jnp.arange(count_slots, dtype=jnp.int32)
    earlier = (brick_helper[:, None] == brick_helper[None, :]) & (slot[None, :] < slot[:, None])
    rank = jnp.sum(earlier.astype(jnp.int32), axis=1)
    target = jnp.where(slot < brick_count[0], brick_helper * capacity + rank, -1)
    code = (brick_anchor[0] * 64 + brick_anchor[1]) * 256 + brick_anchor[2] * 2 + 1
    table_rows = jnp.arange(n * capacity, dtype=jnp.int32)
    codes = jnp.sum(jnp.where(table_rows[:, None] == target[None, :], code[None, :], 0), axis=1)

    keep, curl, sigma, mass = pl.pallas_call(
        material_kernel,
        out_shape=[grid] * 4,
        in_specs=[VMEM_SPEC] * 2,
        out_specs=[VMEM_SPEC] * 4,
        scratch_shapes=[padded, padded],
        compiler_params=params(),
        name="materials",
    )(tables, tissue)

    angles = [2.0 * math.pi * (START + step + 1) / PERIOD for step in range(STEPS)]
    phase = jnp.asarray(np.array([[math.cos(t), math.sin(t)] for t in angles], np.float32))
    wide = pltpu.VMEM((width + 2 * APRON, ny, nz), F32)
    electric, magnetic, sar = pl.pallas_call(
        functools.partial(field_kernel, n),
        out_shape=[fields, fields, grid],
        in_specs=[SMEM_SPEC] + [ANY_SPEC] * 4 + [VMEM_SPEC] * 4,
        out_specs=[ANY_SPEC, ANY_SPEC, VMEM_SPEC],
        scratch_shapes=[
            pltpu.VMEM((3, width, ny + 2 * PAD, nz), F32),
            pltpu.VMEM((3, width, ny + 2 * PAD, nz), F32),
            pltpu.VMEM((3, width, ny, nz), F32),
            pltpu.VMEM((3, width, ny, nz), F32),
            pltpu.VMEM((STEPS, 2, ny, nz), F32),
            pltpu.VMEM((STEPS, 3, ny + PAD, nz), F32),
            pltpu.VMEM((2, ny, nz), F32),
            padded,
            padded,
            wide,
            wide,
            pltpu.SemaphoreType.DMA((4,)),
            pltpu.SemaphoreType.DMA((2,)),
            pltpu.SemaphoreType.DMA((STEPS,)),
            pltpu.SemaphoreType.DMA((STEPS,)),
            pltpu.SemaphoreType.DMA((2,)),
            pltpu.SemaphoreType.DMA((8,)),
        ],
        compiler_params=params(collective_id=0, has_side_effects=True),
        name="fields",
    )(phase, e_field, h_field, phasor_re, phasor_im, keep, curl, sigma, mass)

    edge = BRICK**3
    sar_table = pl.pallas_call(
        functools.partial(brick_kernel, n),
        out_shape=jax.ShapeDtypeStruct((n * capacity, edge), F32),
        in_specs=[SMEM_SPEC, VMEM_SPEC],
        out_specs=VMEM_SPEC,
        scratch_shapes=[
            pltpu.VMEM((n, capacity, edge), F32),
            pltpu.VMEM((n, capacity, edge), F32),
            pltpu.SemaphoreType.DMA((n,)),
            pltpu.SemaphoreType.DMA((n,)),
        ],
        compiler_params=params(collective_id=1, has_side_effects=True),
        name="bricks",
    )(codes, sar)
    return (electric, magnetic, sar_table)


def solution(mesh):
    block = P(None, ("parts", "slab"), None, None)
    layers = P(("parts", "slab"), None, None)
    slots = P(("parts", "slab"))
    return jax.shard_map(
        body,
        mesh=mesh,
        in_specs=(
            block,
            block,
            block,
            block,
            layers,
            P(),
            P(),
            P(),
            P(None, ("parts", "slab")),
            slots,
            slots,
        ),
        out_specs=(block, block, P(("parts", "slab"), None)),
        check_vma=False,
    )
```

```python
import functools
import math

import jax
import jax.numpy as jnp
from jax import lax
from jax.experimental import pallas as pl
from jax.experimental.pallas import tpu as pltpu
from jax.sharding import PartitionSpec as P

STEPS = 6
APRON = 10
BRICK = 8
PERIOD = 2600
START = 325
COURANT = 0.5
FLOOR_SHARE = 0.2
PAD = 8
LANES = 128
F32 = jnp.float32
VMEM_SPEC = pl.BlockSpec(memory_space=pltpu.VMEM)
SMEM_SPEC = pl.BlockSpec(memory_space=pltpu.SMEM)
ANY_SPEC = pl.BlockSpec(memory_space=pl.ANY)
VMEM_LIMIT = 48 * 1024 * 1024


def band(across_z):
    row = lax.broadcasted_iota(jnp.int32, (across_z, across_z), 0)
    col = lax.broadcasted_iota(jnp.int32, (across_z, across_z), 1)
    return (jnp.abs(row - col) <= APRON).astype(F32).astype(jnp.bfloat16)


def along_z(rows, matrix):
    high = rows.astype(jnp.bfloat16)
    rest = rows - high.astype(F32)
    middle = rest.astype(jnp.bfloat16)
    low = (rest - middle.astype(F32)).astype(jnp.bfloat16)
    total = jnp.dot(low, matrix, preferred_element_type=F32)
    total = total + jnp.dot(middle, matrix, preferred_element_type=F32)
    return total + jnp.dot(high, matrix, preferred_element_type=F32)


def clear_margins(padded):
    layers, rows, lanes = padded.shape
    zero = jnp.zeros((layers, 16, lanes), F32)
    padded[:, 0:16] = zero
    padded[:, rows - 16 : rows] = zero


def along_y(padded, triples, layer, across_y):
    count = across_y + 24
    triples[layer, 0:count] = (
        padded[layer, 0:count] + padded[layer, 1 : count + 1] + padded[layer, 2 : count + 2]
    )
    total = triples[layer, 6 : 6 + across_y]
    for part in range(1, 7):
        total = total + triples[layer, 6 + 3 * part : 6 + 3 * part + across_y]
    return total


def window_21(layers, count):
    two = [a + b for a, b in zip(layers[:-1], layers[1:])]
    four = [a + b for a, b in zip(two[:-2], two[2:])]
    eight = [a + b for a, b in zip(four[:-4], four[4:])]
    return [
        (eight[i] + eight[i + 8]) + (four[i + 16] + layers[i + 20]) for i in range(count)
    ]


def material_kernel(
    sigma_ref, eps_ref, density_ref, tissue, keep, curl, sigma, mass, padded, triples, tables
):
    width, across_y, across_z = tissue.shape
    shape = (8, LANES)
    count = sigma_ref.shape[1]
    tables[...] = jnp.zeros_like(tables)
    tables[0:1, 0:count] = sigma_ref[...]
    tables[1:2, 0:count] = eps_ref[...] - 1.0
    tables[2:3, 0:count] = density_ref[...]
    shifted = pltpu.roll(tables[...], 1, 1)
    sig = jnp.broadcast_to(shifted[0:1, :], shape)
    eps = 1.0 + jnp.broadcast_to(shifted[1:2, :], shape)
    rho = jnp.broadcast_to(shifted[2:3, :], shape)
    damping = sig / (2.0 * eps)
    keep_row = (1.0 - damping) / (1.0 + damping)
    curl_row = COURANT / (eps * (1.0 + damping))
    clear_margins(padded)
    matrix = band(across_z)

    def one_layer(layer, carry):
        for y in range(0, across_y, 8):
            ids = tissue[layer, y : y + 8, :]
            keep[layer, y : y + 8, :] = jnp.take_along_axis(keep_row, ids, axis=1)
            curl[layer, y : y + 8, :] = jnp.take_along_axis(curl_row, ids, axis=1)
            sigma[layer, y : y + 8, :] = jnp.take_along_axis(sig, ids, axis=1)
            padded[layer, 16 + y : 24 + y, :] = jnp.take_along_axis(rho, ids, axis=1)
        return carry

    lax.fori_loop(0, width, one_layer, 0)

    def sum_z(group, carry):
        layers = pl.ds(group * 4, 4)
        rows = padded[layers, 16 : 16 + across_y, :].reshape(4 * across_y, across_z)
        padded[layers, 16 : 16 + across_y, :] = along_z(rows, matrix).reshape(
            4, across_y, across_z
        )
        return carry

    lax.fori_loop(0, width // 4, sum_z, 0)

    def sum_y(layer, carry):
        mass[layer] = along_y(padded, triples, layer, across_y)
        return carry

    lax.fori_loop(0, width, sum_y, 0)


def field_kernel(
    n,
    e_in,
    h_in,
    re_in,
    im_in,
    keep,
    curl,
    sigma,
    mass,
    e_out,
    h_out,
    sar,
    E,
    H,
    re,
    im,
    e_hi,
    e_lo,
    h_lo,
    padded,
    triples,
    heat,
    weight,
    local_sem,
    send_sem,
    hi_sem,
    lo_sem,
    first_sem,
    halo_sem,
):
    width, ny, nz = keep.shape
    last = width - 1
    rows = pl.ds(PAD, ny)
    me = lax.axis_index("slab")
    prev = jnp.maximum(me - 1, 0)
    after = jnp.minimum(me + 1, n - 1)
    has_prev = me > 0
    has_next = me < n - 1

    loads = [
        pltpu.make_async_copy(e_in, E.at[:, :, rows], local_sem.at[0]),
        pltpu.make_async_copy(h_in, H.at[:, :, rows], local_sem.at[1]),
        pltpu.make_async_copy(re_in, re, local_sem.at[2]),
        pltpu.make_async_copy(im_in, im, local_sem.at[3]),
    ]
    for copy in loads:
        copy.start()
    margin = jnp.zeros((3, width, PAD, nz), F32)
    for field in (E, H):
        field[:, :, 0:PAD] = margin
        field[:, :, PAD + ny : 2 * PAD + ny] = margin
    e_hi[...] = jnp.zeros_like(e_hi)
    e_lo[...] = jnp.zeros_like(e_lo)
    h_lo[...] = jnp.zeros_like(h_lo)
    apron = jnp.zeros((APRON, ny, nz), F32)
    for block in (heat, weight):
        block[0:APRON] = apron
        block[APRON + width : 2 * APRON + width] = apron
    clear_margins(padded)

    barrier = pltpu.get_barrier_semaphore()

    @pl.when(has_prev)
    def _():
        pl.semaphore_signal(barrier, inc=1, device_id={"slab": prev})

    @pl.when(has_next)
    def _():
        pl.semaphore_signal(barrier, inc=1, device_id={"slab": after})

    pl.semaphore_wait(barrier, has_prev.astype(jnp.int32) + has_next.astype(jnp.int32))

    def down(slot):
        return pltpu.make_async_remote_copy(
            E.at[pl.ds(1, 2), 0, rows], e_hi.at[slot], send_sem.at[0], hi_sem.at[slot],
            device_id={"slab": prev},
        )

    def up(slot):
        return pltpu.make_async_remote_copy(
            E.at[:, last, rows], e_lo.at[slot, :, pl.ds(0, ny)], send_sem.at[1], lo_sem.at[slot],
            device_id={"slab": after},
        )

    first = pltpu.make_async_remote_copy(
        H.at[pl.ds(1, 2), last, rows], h_lo, first_sem.at[0], first_sem.at[1],
        device_id={"slab": after},
    )

    def halo_down(block, at, start=0, count=APRON):
        return pltpu.make_async_remote_copy(
            block.at[pl.ds(APRON + start, count)],
            block.at[pl.ds(APRON + width + start, count)],
            halo_sem.at[at], halo_sem.at[at + 1], device_id={"slab": prev},
        )

    def halo_up(block, at, start=0, count=APRON):
        return pltpu.make_async_remote_copy(
            block.at[pl.ds(width + start, count)], block.at[pl.ds(start, count)],
            halo_sem.at[at + 2], halo_sem.at[at + 3], device_id={"slab": after},
        )

    loads[0].wait()
    loads[1].wait()

    @pl.when(has_prev)
    def _():
        down(0).start()

    @pl.when(has_next)
    def _():
        up(0).start()
        first.start()

    weight[APRON : APRON + width] = mass[...]

    lane = lax.broadcasted_iota(jnp.int32, (ny, nz), 1)
    not_last = (lane < nz - 1).astype(F32)
    not_first = (lane > 0).astype(F32)

    def z_up(a):
        return pltpu.roll(a, nz - 1, 1) * not_last

    def z_down(a):
        return pltpu.roll(a, 1, 1) * not_first

    def body_of(field, part, layer):
        return field[part, layer, PAD : PAD + ny]

    def y_up(field, part, layer):
        return field[part, layer, PAD + 1 : PAD + 1 + ny]

    def y_down(field, part, layer):
        return field[part, layer, PAD - 1 : PAD - 1 + ny]

    def put(field, part, layer, value):
        field[part, layer, PAD : PAD + ny] = value

    def magnetic(layer, ey_next, ez_next):
        ex, ey, ez = (body_of(E, part, layer) for part in range(3))
        put(H, 0, layer, body_of(H, 0, layer)
            - COURANT * ((y_up(E, 2, layer) - ez) - (z_up(ey) - ey)))
        put(H, 1, layer, body_of(H, 1, layer)
            - COURANT * ((z_up(ex) - ex) - (ez_next - ez)))
        put(H, 2, layer, body_of(H, 2, layer)
            - COURANT * ((ey_next - ey) - (y_up(E, 0, layer) - ex)))

    def magnetic_at(layer):
        magnetic(layer, body_of(E, 1, layer + 1), body_of(E, 2, layer + 1))

    def electric(layer, hy_prev, hz_prev):
        hx, hy, hz = (body_of(H, part, layer) for part in range(3))
        k, c = (keep[layer], curl[layer])
        ex = k * body_of(E, 0, layer) + c * ((hz - y_down(H, 2, layer)) - (hy - z_down(hy)))
        put(E, 0, layer, ex)
        ey = k * body_of(E, 1, layer) + c * ((hx - z_down(hx)) - (hz - hz_prev))
        put(E, 1, layer, ey)
        ez = k * body_of(E, 2, layer) + c * ((hy - hy_prev) - (hx - y_down(H, 0, layer)))
        put(E, 2, layer, ez)

    def electric_at(layer):
        electric(layer, body_of(H, 1, layer - 1), body_of(H, 2, layer - 1))

    def by_step(step, values):
        value = jnp.float32(values[0])
        for at in range(1, STEPS):
            value = jnp.where(step == at, jnp.float32(values[at]), value)
        return value

    angles = [2.0 * math.pi * (START + at + 1) / PERIOD for at in range(STEPS)]

    def phasor(step, layer, real, imag):
        for part in range(3):
            value = body_of(E, part, layer)
            re[part, layer] = re[part, layer] + real * value
            im[part, layer] = im[part, layer] - imag * value

    live = has_prev.astype(F32)

    def one_step(step, carry):
        @pl.when(has_next)
        def _():
            down(step).wait_recv()

        @pl.when(has_prev)
        def _():
            up(step).wait_recv()

        @pl.when(has_prev & (step == 0))
        def _():
            first.wait_recv()

        real = by_step(step, [math.cos(t) for t in angles])
        imag = by_step(step, [math.sin(t) for t in angles])
        ex = e_lo[step, 0, 0:ny]
        h_lo[0] = live * (
            h_lo[0]
            - COURANT * ((z_up(ex) - ex) - (body_of(E, 2, 0) - e_lo[step, 2, 0:ny]))
        )
        h_lo[1] = live * (
            h_lo[1]
            - COURANT
            * ((body_of(E, 1, 0) - e_lo[step, 1, 0:ny]) - (e_lo[step, 0, 1 : ny + 1] - ex))
        )
        @pl.when(has_next & (step == 0))
        def _():
            first.wait_send()

        magnetic_at(0)
        magnetic_at(last - 1)
        magnetic(last, e_hi[step, 0], e_hi[step, 1])

        @pl.when(has_prev)
        def _():
            down(step).wait_send()

        @pl.when(has_next)
        def _():
            up(step).wait_send()

        electric(0, h_lo[0], h_lo[1])
        electric_at(last)

        @pl.when(has_prev & (step < STEPS - 1))
        def _():
            down(step + 1).start()
            halo_down(weight, 4, 2 * step, 2).start()

        @pl.when(has_next & (step < STEPS - 1))
        def _():
            up(step + 1).start()
            halo_up(weight, 4, 2 * step, 2).start()

        @pl.when(step == 0)
        def _():
            loads[2].wait()
            loads[3].wait()

        def inner(layer, carry):
            magnetic_at(layer)
            electric_at(layer)
            phasor(step, layer, real, imag)
            return carry

        lax.fori_loop(1, last - 1, inner, 0)
        electric_at(last - 1)
        phasor(step, last - 1, real, imag)
        phasor(step, 0, real, imag)
        phasor(step, last, real, imag)
        return carry

    lax.fori_loop(0, STEPS, one_step, 0)

    stores = [
        pltpu.make_async_copy(E.at[:, :, rows], e_out, local_sem.at[0]),
        pltpu.make_async_copy(H.at[:, :, rows], h_out, local_sem.at[1]),
    ]
    for copy in stores:
        copy.start()

    matrix = band(nz)

    def heat_group(base):
        layers = pl.ds(base, 4)
        total = jnp.zeros((4, ny, nz), F32)
        for part in range(3):
            real, imag = (re[part, layers], im[part, layers])
            total = total + (real * real + imag * imag)
        total = (0.5 * sigma[layers]) * total
        padded[layers, 16 : 16 + ny, :] = along_z(total.reshape(4 * ny, nz), matrix).reshape(
            4, ny, nz
        )
        for layer in range(4):
            heat[APRON + base + layer] = along_y(padded, triples, base + layer, ny)

    def send_down(start, end):
        @pl.when(has_prev)
        def _():
            halo_down(heat, 0, start, end - start).start()

    def send_up(start, end):
        @pl.when(has_next)
        def _():
            halo_up(heat, 0, start, end - start).start()

    groups = width // 4
    for base in [0, width - 4] + [4 * i for i in range(1, groups - 1)]:
        heat_group(base)
        if base < APRON:
            send_down(base, min(base + 4, APRON))
        if base + 4 > width - APRON:
            send_up(max(base - (width - APRON), 0), base + 4 - (width - APRON))

    @pl.when(has_prev)
    def _():
        halo_down(weight, 4).wait_send()

    @pl.when(has_next)
    def _():
        halo_up(weight, 4).wait_send()
        halo_down(weight, 4).wait_recv()

    @pl.when(has_prev)
    def _():
        halo_up(weight, 4).wait_recv()

    floor_mass = FLOOR_SHARE * (2 * APRON + 1) ** 3

    def weigh(block, carry):
        at = pl.ds(pl.multiple_of(block * 8, 8), 8)
        sums = window_21([weight[i, at] for i in range(width + 2 * APRON)], width)
        for i in range(width):
            sar[i, at] = 1.0 / jnp.maximum(sums[i], floor_mass)
        return carry

    lax.fori_loop(0, ny // 8, weigh, 0)

    @pl.when(has_prev)
    def _():
        halo_down(heat, 0).wait_send()
        halo_up(heat, 0).wait_recv()

    @pl.when(has_next)
    def _():
        halo_up(heat, 0).wait_send()
        halo_down(heat, 0).wait_recv()

    def average(block, carry):
        at = pl.ds(pl.multiple_of(block * 8, 8), 8)
        sums = window_21([heat[i, at] for i in range(width + 2 * APRON)], width)
        for i in range(width):
            sar[i, at] = sums[i] * sar[i, at]
        return carry

    lax.fori_loop(0, ny // 8, average, 0)
    for copy in stores:
        copy.wait()


def brick_kernel(n, codes, sar, table, outgoing, landed, send_sem, recv_sem):
    capacity = outgoing.shape[1] // 4
    me = lax.axis_index("slab")
    barrier = pltpu.get_barrier_semaphore()

    def greet(k, carry):
        pl.semaphore_signal(barrier, inc=1, device_id={"slab": lax.rem(me + k, n)})
        return carry

    lax.fori_loop(1, n, greet, 0)

    shape = (8, LANES)
    lane = lax.broadcasted_iota(jnp.int32, shape, 1)
    sub = lax.broadcasted_iota(jnp.int32, shape, 0)
    even = ((lane - 8 * sub) >= 0) & ((lane - 8 * sub) < 8)
    odd = ((lane - 8 * sub) >= 64) & ((lane - 8 * sub) < 72)

    def one_row(helper, rank):
        code = codes[helper * capacity + rank]
        z = lax.bitwise_and(lax.shift_right_logical(code, 1), 127)
        y = lax.bitwise_and(lax.shift_right_logical(code, 8), 63)
        x = lax.shift_right_logical(code, 14)
        listed = lax.bitwise_and(code, 1).astype(F32)
        from_even = lax.bitwise_and(lane - 8 * sub + z, LANES - 1)
        from_odd = lax.bitwise_and(lane - 8 * sub + (z + 64), LANES - 1)
        for pair in range(BRICK // 2):
            first = jnp.take_along_axis(sar[x + 2 * pair, pl.ds(y, 8), :], from_even, axis=1)
            second = jnp.take_along_axis(sar[x + 2 * pair + 1, pl.ds(y, 8), :], from_odd, axis=1)
            both = jnp.where(even, first, jnp.where(odd, second, 0.0))
            outgoing[helper, pl.ds(4 * rank + pair, 1), :] = listed * jnp.sum(
                both, axis=0, keepdims=True
            )

    def fill(helper):
        for rank in range(capacity):
            one_row(helper, rank)

    def copy_to(k):
        helper = lax.rem(me + k, n)
        return pltpu.make_async_remote_copy(
            outgoing.at[helper], landed.at[me], send_sem.at[k], recv_sem.at[me],
            device_id={"slab": helper},
        )

    fill(lax.rem(me + 1, n))
    pl.semaphore_wait(barrier, n - 1)
    copy_to(1).start()

    def send(k, carry):
        fill(lax.rem(me + k, n))
        copy_to(k).start()
        return carry

    lax.fori_loop(2, n, send, 0)
    fill(me)
    landed[me] = outgoing[me]

    def finish(k, carry):
        copy_to(k).wait_send()
        source = lax.rem(me + k, n)
        pltpu.make_async_remote_copy(
            outgoing.at[source], landed.at[source], send_sem.at[k], recv_sem.at[source],
            device_id={"slab": source},
        ).wait_recv()
        return carry

    lax.fori_loop(1, n, finish, 0)
    for source in range(n):
        at = slice(source * capacity, (source + 1) * capacity)
        for pair in range(BRICK // 2):
            table[at, pair * LANES : (pair + 1) * LANES] = landed[
                source, pl.ds(pair, capacity, stride=4), :
            ]


def body(
    e_field,
    h_field,
    phasor_re,
    phasor_im,
    tissue,
    sigma_table,
    eps_table,
    density_table,
    brick_anchor,
    brick_helper,
    brick_count,
):
    width, ny, nz = tissue.shape
    n = lax.axis_size("slab")
    grid = jax.ShapeDtypeStruct((width, ny, nz), F32)
    fields = jax.ShapeDtypeStruct(e_field.shape, F32)
    padded = pltpu.VMEM((width, ny + 32, nz), F32)
    params = functools.partial(pltpu.CompilerParams, vmem_limit_bytes=VMEM_LIMIT)

    count_slots = brick_helper.shape[0]
    capacity = max(2, (count_slots + n - 1) // n)
    slot = jnp.arange(count_slots, dtype=jnp.int32)
    earlier = (brick_helper[:, None] == brick_helper[None, :]) & (slot[None, :] < slot[:, None])
    rank = jnp.sum(earlier.astype(jnp.int32), axis=1)
    target = jnp.where(slot < brick_count[0], brick_helper * capacity + rank, -1)
    code = (brick_anchor[0] * 64 + brick_anchor[1]) * 256 + brick_anchor[2] * 2 + 1
    table_rows = jnp.arange(n * capacity, dtype=jnp.int32)
    codes = jnp.sum(jnp.where(table_rows[:, None] == target[None, :], code[None, :], 0), axis=1)

    keep, curl, sigma, mass = pl.pallas_call(
        material_kernel,
        out_shape=[grid] * 4,
        in_specs=[VMEM_SPEC] * 4,
        out_specs=[VMEM_SPEC] * 4,
        scratch_shapes=[padded, padded, pltpu.VMEM((8, LANES), F32)],
        compiler_params=params(),
        name="materials",
    )(sigma_table[None, :], eps_table[None, :], density_table[None, :], tissue)

    wide = pltpu.VMEM((width + 2 * APRON, ny, nz), F32)
    electric, magnetic, sar = pl.pallas_call(
        functools.partial(field_kernel, n),
        out_shape=[fields, fields, grid],
        in_specs=[ANY_SPEC] * 4 + [VMEM_SPEC] * 4,
        out_specs=[ANY_SPEC, ANY_SPEC, VMEM_SPEC],
        scratch_shapes=[
            pltpu.VMEM((3, width, ny + 2 * PAD, nz), F32),
            pltpu.VMEM((3, width, ny + 2 * PAD, nz), F32),
            pltpu.VMEM((3, width, ny, nz), F32),
            pltpu.VMEM((3, width, ny, nz), F32),
            pltpu.VMEM((STEPS, 2, ny, nz), F32),
            pltpu.VMEM((STEPS, 3, ny + PAD, nz), F32),
            pltpu.VMEM((2, ny, nz), F32),
            padded,
            padded,
            wide,
            wide,
            pltpu.SemaphoreType.DMA((4,)),
            pltpu.SemaphoreType.DMA((2,)),
            pltpu.SemaphoreType.DMA((STEPS,)),
            pltpu.SemaphoreType.DMA((STEPS,)),
            pltpu.SemaphoreType.DMA((2,)),
            pltpu.SemaphoreType.DMA((8,)),
        ],
        compiler_params=params(collective_id=0, has_side_effects=True),
        name="fields",
    )(e_field, h_field, phasor_re, phasor_im, keep, curl, sigma, mass)

    edge = BRICK**3
    sar_table = pl.pallas_call(
        functools.partial(brick_kernel, n),
        out_shape=jax.ShapeDtypeStruct((n * capacity, edge), F32),
        in_specs=[SMEM_SPEC, VMEM_SPEC],
        out_specs=VMEM_SPEC,
        scratch_shapes=[
            pltpu.VMEM((n, 4 * capacity, LANES), F32),
            pltpu.VMEM((n, 4 * capacity, LANES), F32),
            pltpu.SemaphoreType.DMA((n,)),
            pltpu.SemaphoreType.DMA((n,)),
        ],
        compiler_params=params(collective_id=1, has_side_effects=True),
        name="bricks",
    )(codes, sar)
    return (electric, magnetic, sar_table)


def solution(mesh):
    block = P(None, ("parts", "slab"), None, None)
    layers = P(("parts", "slab"), None, None)
    slots = P(("parts", "slab"))
    return jax.shard_map(
        body,
        mesh=mesh,
        in_specs=(
            block,
            block,
            block,
            block,
            layers,
            P(),
            P(),
            P(),
            P(None, ("parts", "slab")),
            slots,
            slots,
        ),
        out_specs=(block, block, P(("parts", "slab"), None)),
        check_vma=False,
    )
```

```python
import functools
import math

import jax
import jax.numpy as jnp
from jax import lax
from jax.experimental import pallas as pl
from jax.experimental.pallas import tpu as pltpu
from jax.sharding import PartitionSpec as P

STEPS = 6
APRON = 10
BRICK = 8
PERIOD = 2600
START = 325
COURANT = 0.5
FLOOR_SHARE = 0.2
PAD = 8
LANES = 128
F32 = jnp.float32
VMEM_SPEC = pl.BlockSpec(memory_space=pltpu.VMEM)
SMEM_SPEC = pl.BlockSpec(memory_space=pltpu.SMEM)
ANY_SPEC = pl.BlockSpec(memory_space=pl.ANY)
VMEM_LIMIT = 48 * 1024 * 1024


def band(across_z):
    row = lax.broadcasted_iota(jnp.int32, (across_z, across_z), 0)
    col = lax.broadcasted_iota(jnp.int32, (across_z, across_z), 1)
    return (jnp.abs(row - col) <= APRON).astype(F32).astype(jnp.bfloat16)


def along_z(rows, matrix):
    high = rows.astype(jnp.bfloat16)
    rest = rows - high.astype(F32)
    middle = rest.astype(jnp.bfloat16)
    low = (rest - middle.astype(F32)).astype(jnp.bfloat16)
    total = jnp.dot(low, matrix, preferred_element_type=F32)
    total = total + jnp.dot(middle, matrix, preferred_element_type=F32)
    return total + jnp.dot(high, matrix, preferred_element_type=F32)


def clear_margins(padded):
    layers, rows, lanes = padded.shape
    zero = jnp.zeros((layers, 16, lanes), F32)
    padded[:, 0:16] = zero
    padded[:, rows - 16 : rows] = zero


def along_y(padded, triples, layer, across_y):
    count = across_y + 24
    triples[layer, 0:count] = (
        padded[layer, 0:count] + padded[layer, 1 : count + 1] + padded[layer, 2 : count + 2]
    )
    total = triples[layer, 6 : 6 + across_y]
    for part in range(1, 7):
        total = total + triples[layer, 6 + 3 * part : 6 + 3 * part + across_y]
    return total


def window_21(layers, count):
    two = [a + b for a, b in zip(layers[:-1], layers[1:])]
    four = [a + b for a, b in zip(two[:-2], two[2:])]
    eight = [a + b for a, b in zip(four[:-4], four[4:])]
    return [
        (eight[i] + eight[i + 8]) + (four[i + 16] + layers[i + 20]) for i in range(count)
    ]


def materials(
    sigma_ref, eps_ref, density_ref, tissue, keep, curl, sigma, mass, padded, triples, tables
):
    width, across_y, across_z = tissue.shape
    shape = (8, LANES)
    count = sigma_ref.shape[1]
    tables[...] = jnp.zeros_like(tables)
    tables[0:1, 0:count] = sigma_ref[...]
    tables[1:2, 0:count] = eps_ref[...] - 1.0
    tables[2:3, 0:count] = density_ref[...]
    shifted = pltpu.roll(tables[...], 1, 1)
    sig = jnp.broadcast_to(shifted[0:1, :], shape)
    eps = 1.0 + jnp.broadcast_to(shifted[1:2, :], shape)
    rho = jnp.broadcast_to(shifted[2:3, :], shape)
    damping = sig / (2.0 * eps)
    keep_row = (1.0 - damping) / (1.0 + damping)
    curl_row = COURANT / (eps * (1.0 + damping))
    clear_margins(padded)
    matrix = band(across_z)

    def one_layer(layer, carry):
        for y in range(0, across_y, 8):
            ids = tissue[layer, y : y + 8, :]
            keep[layer, y : y + 8, :] = jnp.take_along_axis(keep_row, ids, axis=1)
            curl[layer, y : y + 8, :] = jnp.take_along_axis(curl_row, ids, axis=1)
            sigma[layer, y : y + 8, :] = jnp.take_along_axis(sig, ids, axis=1)
            padded[layer, 16 + y : 24 + y, :] = jnp.take_along_axis(rho, ids, axis=1)
        return carry

    lax.fori_loop(0, width, one_layer, 0)

    def sum_z(group, carry):
        layers = pl.ds(group * 4, 4)
        rows = padded[layers, 16 : 16 + across_y, :].reshape(4 * across_y, across_z)
        padded[layers, 16 : 16 + across_y, :] = along_z(rows, matrix).reshape(
            4, across_y, across_z
        )
        return carry

    lax.fori_loop(0, width // 4, sum_z, 0)

    def sum_y(layer, carry):
        mass[layer] = along_y(padded, triples, layer, across_y)
        return carry

    lax.fori_loop(0, width, sum_y, 0)


def field_kernel(
    n,
    codes,
    sigma_in,
    eps_in,
    density_in,
    tissue_in,
    e_in,
    h_in,
    re_in,
    im_in,
    e_out,
    h_out,
    table,
    sigma_row,
    eps_row,
    density_row,
    tissue,
    tables,
    keep,
    curl,
    sigma,
    sar,
    outgoing,
    landed,
    row_send,
    row_recv,
    E,
    H,
    re,
    im,
    e_hi,
    e_lo,
    h_lo,
    padded,
    triples,
    heat,
    weight,
    local_sem,
    send_sem,
    hi_sem,
    lo_sem,
    first_sem,
    halo_sem,
):
    width, ny, nz = tissue.shape
    last = width - 1
    rows = pl.ds(PAD, ny)
    me = lax.axis_index("slab")
    prev = jnp.maximum(me - 1, 0)
    after = jnp.minimum(me + 1, n - 1)
    has_prev = me > 0
    has_next = me < n - 1

    loads = [
        pltpu.make_async_copy(e_in, E.at[:, :, rows], local_sem.at[0]),
        pltpu.make_async_copy(h_in, H.at[:, :, rows], local_sem.at[1]),
        pltpu.make_async_copy(re_in, re, local_sem.at[2]),
        pltpu.make_async_copy(im_in, im, local_sem.at[3]),
        pltpu.make_async_copy(sigma_in, sigma_row, local_sem.at[4]),
        pltpu.make_async_copy(eps_in, eps_row, local_sem.at[5]),
        pltpu.make_async_copy(density_in, density_row, local_sem.at[6]),
        pltpu.make_async_copy(tissue_in, tissue, local_sem.at[7]),
    ]
    for copy in loads:
        copy.start()
    margin = jnp.zeros((3, width, PAD, nz), F32)
    for field in (E, H):
        field[:, :, 0:PAD] = margin
        field[:, :, PAD + ny : 2 * PAD + ny] = margin
    e_hi[...] = jnp.zeros_like(e_hi)
    e_lo[...] = jnp.zeros_like(e_lo)
    h_lo[...] = jnp.zeros_like(h_lo)
    apron = jnp.zeros((APRON, ny, nz), F32)
    for block in (heat, weight):
        block[0:APRON] = apron
        block[APRON + width : 2 * APRON + width] = apron

    barrier = pltpu.get_barrier_semaphore()

    def greet(k, carry):
        pl.semaphore_signal(barrier, inc=1, device_id={"slab": lax.rem(me + k, n)})
        return carry

    lax.fori_loop(1, n, greet, 0)
    pl.semaphore_wait(barrier, n - 1)

    def down(slot):
        return pltpu.make_async_remote_copy(
            E.at[pl.ds(1, 2), 0, rows], e_hi.at[slot], send_sem.at[0], hi_sem.at[slot],
            device_id={"slab": prev},
        )

    def up(slot):
        return pltpu.make_async_remote_copy(
            E.at[:, last, rows], e_lo.at[slot, :, pl.ds(0, ny)], send_sem.at[1], lo_sem.at[slot],
            device_id={"slab": after},
        )

    first = pltpu.make_async_remote_copy(
        H.at[pl.ds(1, 2), last, rows], h_lo, first_sem.at[0], first_sem.at[1],
        device_id={"slab": after},
    )

    def halo_down(block, at, start=0, count=APRON):
        return pltpu.make_async_remote_copy(
            block.at[pl.ds(APRON + start, count)],
            block.at[pl.ds(APRON + width + start, count)],
            halo_sem.at[at], halo_sem.at[at + 1], device_id={"slab": prev},
        )

    def halo_up(block, at, start=0, count=APRON):
        return pltpu.make_async_remote_copy(
            block.at[pl.ds(width + start, count)], block.at[pl.ds(start, count)],
            halo_sem.at[at + 2], halo_sem.at[at + 3], device_id={"slab": after},
        )

    loads[0].wait()
    loads[1].wait()

    @pl.when(has_prev)
    def _():
        down(0).start()

    @pl.when(has_next)
    def _():
        up(0).start()
        first.start()

    for copy in loads[4:]:
        copy.wait()
    materials(
        sigma_row, eps_row, density_row, tissue, keep, curl, sigma,
        weight.at[pl.ds(APRON, width)], padded, triples, tables,
    )

    lane = lax.broadcasted_iota(jnp.int32, (ny, nz), 1)
    not_last = (lane < nz - 1).astype(F32)
    not_first = (lane > 0).astype(F32)

    def z_up(a):
        return pltpu.roll(a, nz - 1, 1) * not_last

    def z_down(a):
        return pltpu.roll(a, 1, 1) * not_first

    def body_of(field, part, layer):
        return field[part, layer, PAD : PAD + ny]

    def y_up(field, part, layer):
        return field[part, layer, PAD + 1 : PAD + 1 + ny]

    def y_down(field, part, layer):
        return field[part, layer, PAD - 1 : PAD - 1 + ny]

    def put(field, part, layer, value):
        field[part, layer, PAD : PAD + ny] = value

    def magnetic(layer, ey_next, ez_next):
        ex, ey, ez = (body_of(E, part, layer) for part in range(3))
        put(H, 0, layer, body_of(H, 0, layer)
            - COURANT * ((y_up(E, 2, layer) - ez) - (z_up(ey) - ey)))
        put(H, 1, layer, body_of(H, 1, layer)
            - COURANT * ((z_up(ex) - ex) - (ez_next - ez)))
        put(H, 2, layer, body_of(H, 2, layer)
            - COURANT * ((ey_next - ey) - (y_up(E, 0, layer) - ex)))

    def magnetic_at(layer):
        magnetic(layer, body_of(E, 1, layer + 1), body_of(E, 2, layer + 1))

    def electric(layer, hy_prev, hz_prev):
        hx, hy, hz = (body_of(H, part, layer) for part in range(3))
        k, c = (keep[layer], curl[layer])
        ex = k * body_of(E, 0, layer) + c * ((hz - y_down(H, 2, layer)) - (hy - z_down(hy)))
        put(E, 0, layer, ex)
        ey = k * body_of(E, 1, layer) + c * ((hx - z_down(hx)) - (hz - hz_prev))
        put(E, 1, layer, ey)
        ez = k * body_of(E, 2, layer) + c * ((hy - hy_prev) - (hx - y_down(H, 0, layer)))
        put(E, 2, layer, ez)

    def electric_at(layer):
        electric(layer, body_of(H, 1, layer - 1), body_of(H, 2, layer - 1))

    def by_step(step, values):
        value = jnp.float32(values[0])
        for at in range(1, STEPS):
            value = jnp.where(step == at, jnp.float32(values[at]), value)
        return value

    angles = [2.0 * math.pi * (START + at + 1) / PERIOD for at in range(STEPS)]

    def phasor(step, layer, real, imag):
        for part in range(3):
            value = body_of(E, part, layer)
            re[part, layer] = re[part, layer] + real * value
            im[part, layer] = im[part, layer] - imag * value

    live = has_prev.astype(F32)

    def one_step(step, carry):
        @pl.when(has_next)
        def _():
            down(step).wait_recv()

        @pl.when(has_prev)
        def _():
            up(step).wait_recv()

        @pl.when(has_prev & (step == 0))
        def _():
            first.wait_recv()

        real = by_step(step, [math.cos(t) for t in angles])
        imag = by_step(step, [math.sin(t) for t in angles])
        ex = e_lo[step, 0, 0:ny]
        h_lo[0] = live * (
            h_lo[0]
            - COURANT * ((z_up(ex) - ex) - (body_of(E, 2, 0) - e_lo[step, 2, 0:ny]))
        )
        h_lo[1] = live * (
            h_lo[1]
            - COURANT
            * ((body_of(E, 1, 0) - e_lo[step, 1, 0:ny]) - (e_lo[step, 0, 1 : ny + 1] - ex))
        )
        @pl.when(has_next & (step == 0))
        def _():
            first.wait_send()

        magnetic_at(0)
        magnetic_at(last - 1)
        magnetic(last, e_hi[step, 0], e_hi[step, 1])

        @pl.when(has_prev)
        def _():
            down(step).wait_send()

        @pl.when(has_next)
        def _():
            up(step).wait_send()

        electric(0, h_lo[0], h_lo[1])
        electric_at(last)

        @pl.when(has_prev & (step < STEPS - 1))
        def _():
            down(step + 1).start()
            halo_down(weight, 4, 2 * step, 2).start()

        @pl.when(has_next & (step < STEPS - 1))
        def _():
            up(step + 1).start()
            halo_up(weight, 4, 2 * step, 2).start()

        @pl.when(step == 0)
        def _():
            loads[2].wait()
            loads[3].wait()

        def inner(layer, carry):
            magnetic_at(layer)
            electric_at(layer)
            phasor(step, layer, real, imag)
            return carry

        lax.fori_loop(1, last - 1, inner, 0)
        electric_at(last - 1)
        phasor(step, last - 1, real, imag)
        phasor(step, 0, real, imag)
        phasor(step, last, real, imag)
        return carry

    lax.fori_loop(0, STEPS, one_step, 0)

    stores = [
        pltpu.make_async_copy(E.at[:, :, rows], e_out, local_sem.at[0]),
        pltpu.make_async_copy(H.at[:, :, rows], h_out, local_sem.at[1]),
    ]
    for copy in stores:
        copy.start()

    matrix = band(nz)

    def heat_group(base):
        layers = pl.ds(base, 4)
        total = jnp.zeros((4, ny, nz), F32)
        for part in range(3):
            real, imag = (re[part, layers], im[part, layers])
            total = total + (real * real + imag * imag)
        total = (0.5 * sigma[layers]) * total
        padded[layers, 16 : 16 + ny, :] = along_z(total.reshape(4 * ny, nz), matrix).reshape(
            4, ny, nz
        )
        for layer in range(4):
            heat[APRON + base + layer] = along_y(padded, triples, base + layer, ny)

    def send_down(start, end):
        @pl.when(has_prev)
        def _():
            halo_down(heat, 0, start, end - start).start()

    def send_up(start, end):
        @pl.when(has_next)
        def _():
            halo_up(heat, 0, start, end - start).start()

    groups = width // 4
    for base in [0, width - 4] + [4 * i for i in range(1, groups - 1)]:
        heat_group(base)
        if base < APRON:
            send_down(base, min(base + 4, APRON))
        if base + 4 > width - APRON:
            send_up(max(base - (width - APRON), 0), base + 4 - (width - APRON))

    @pl.when(has_prev)
    def _():
        halo_down(weight, 4).wait_send()

    @pl.when(has_next)
    def _():
        halo_up(weight, 4).wait_send()
        halo_down(weight, 4).wait_recv()

    @pl.when(has_prev)
    def _():
        halo_up(weight, 4).wait_recv()

    floor_mass = FLOOR_SHARE * (2 * APRON + 1) ** 3

    def weigh(block, carry):
        at = pl.ds(pl.multiple_of(block * 8, 8), 8)
        sums = window_21([weight[i, at] for i in range(width + 2 * APRON)], width)
        for i in range(width):
            sar[i, at] = 1.0 / jnp.maximum(sums[i], floor_mass)
        return carry

    lax.fori_loop(0, ny // 8, weigh, 0)

    @pl.when(has_prev)
    def _():
        halo_down(heat, 0).wait_send()
        halo_up(heat, 0).wait_recv()

    @pl.when(has_next)
    def _():
        halo_up(heat, 0).wait_send()
        halo_down(heat, 0).wait_recv()

    def average(block, carry):
        at = pl.ds(pl.multiple_of(block * 8, 8), 8)
        sums = window_21([heat[i, at] for i in range(width + 2 * APRON)], width)
        for i in range(width):
            sar[i, at] = sums[i] * sar[i, at]
        return carry

    lax.fori_loop(0, ny // 8, average, 0)
    send_bricks(n, codes, sar, table, outgoing, landed, row_send, row_recv)
    for copy in stores:
        copy.wait()


def send_bricks(n, codes, sar, table, outgoing, landed, send_sem, recv_sem):
    capacity = outgoing.shape[1] // 4
    me = lax.axis_index("slab")
    shape = (8, LANES)
    lane = lax.broadcasted_iota(jnp.int32, shape, 1)
    sub = lax.broadcasted_iota(jnp.int32, shape, 0)
    even = ((lane - 8 * sub) >= 0) & ((lane - 8 * sub) < 8)
    odd = ((lane - 8 * sub) >= 64) & ((lane - 8 * sub) < 72)

    def one_row(helper, rank):
        code = codes[helper * capacity + rank]
        z = lax.bitwise_and(lax.shift_right_logical(code, 1), 127)
        y = lax.bitwise_and(lax.shift_right_logical(code, 8), 63)
        x = lax.shift_right_logical(code, 14)
        listed = lax.bitwise_and(code, 1).astype(F32)
        from_even = lax.bitwise_and(lane - 8 * sub + z, LANES - 1)
        from_odd = lax.bitwise_and(lane - 8 * sub + (z + 64), LANES - 1)
        for pair in range(BRICK // 2):
            first = jnp.take_along_axis(sar[x + 2 * pair, pl.ds(y, 8), :], from_even, axis=1)
            second = jnp.take_along_axis(sar[x + 2 * pair + 1, pl.ds(y, 8), :], from_odd, axis=1)
            both = jnp.where(even, first, jnp.where(odd, second, 0.0))
            outgoing[helper, pl.ds(4 * rank + pair, 1), :] = listed * jnp.sum(
                both, axis=0, keepdims=True
            )

    def fill(helper):
        for rank in range(capacity):
            one_row(helper, rank)

    def copy_to(k):
        helper = lax.rem(me + k, n)
        return pltpu.make_async_remote_copy(
            outgoing.at[helper], landed.at[me], send_sem.at[k], recv_sem.at[me],
            device_id={"slab": helper},
        )

    fill(lax.rem(me + 1, n))
    copy_to(1).start()

    def send(k, carry):
        fill(lax.rem(me + k, n))
        copy_to(k).start()
        return carry

    lax.fori_loop(2, n, send, 0)
    fill(me)
    landed[me] = outgoing[me]

    def finish(k, carry):
        copy_to(k).wait_send()
        source = lax.rem(me + k, n)
        pltpu.make_async_remote_copy(
            outgoing.at[source], landed.at[source], send_sem.at[k], recv_sem.at[source],
            device_id={"slab": source},
        ).wait_recv()
        return carry

    lax.fori_loop(1, n, finish, 0)
    for source in range(n):
        at = slice(source * capacity, (source + 1) * capacity)
        for pair in range(BRICK // 2):
            table[at, pair * LANES : (pair + 1) * LANES] = landed[
                source, pl.ds(pair, capacity, stride=4), :
            ]


def body(
    e_field,
    h_field,
    phasor_re,
    phasor_im,
    tissue,
    sigma_table,
    eps_table,
    density_table,
    brick_anchor,
    brick_helper,
    brick_count,
):
    width, ny, nz = tissue.shape
    n = lax.axis_size("slab")
    fields = jax.ShapeDtypeStruct(e_field.shape, F32)
    padded = pltpu.VMEM((width, ny + 32, nz), F32)
    params = functools.partial(pltpu.CompilerParams, vmem_limit_bytes=VMEM_LIMIT)

    count_slots = brick_helper.shape[0]
    capacity = max(2, (count_slots + n - 1) // n)
    slot = jnp.arange(count_slots, dtype=jnp.int32)
    earlier = (brick_helper[:, None] == brick_helper[None, :]) & (slot[None, :] < slot[:, None])
    rank = jnp.sum(earlier.astype(jnp.int32), axis=1)
    target = jnp.where(slot < brick_count[0], brick_helper * capacity + rank, -1)
    code = (brick_anchor[0] * 64 + brick_anchor[1]) * 256 + brick_anchor[2] * 2 + 1
    table_rows = jnp.arange(n * capacity, dtype=jnp.int32)
    codes = jnp.sum(jnp.where(table_rows[:, None] == target[None, :], code[None, :], 0), axis=1)

    wide = pltpu.VMEM((width + 2 * APRON, ny, nz), F32)
    block = pltpu.VMEM((width, ny, nz), F32)
    entries = pltpu.VMEM((1, sigma_table.shape[0]), F32)
    rows = pltpu.VMEM((n, 4 * capacity, LANES), F32)
    return pl.pallas_call(
        functools.partial(field_kernel, n),
        out_shape=[fields, fields, jax.ShapeDtypeStruct((n * capacity, BRICK**3), F32)],
        in_specs=[SMEM_SPEC] + [ANY_SPEC] * 8,
        out_specs=[ANY_SPEC, ANY_SPEC, VMEM_SPEC],
        scratch_shapes=[
            entries,
            entries,
            entries,
            pltpu.VMEM((width, ny, nz), jnp.int32),
            pltpu.VMEM((8, LANES), F32),
            block,
            block,
            block,
            block,
            rows,
            rows,
            pltpu.SemaphoreType.DMA((n,)),
            pltpu.SemaphoreType.DMA((n,)),
            pltpu.VMEM((3, width, ny + 2 * PAD, nz), F32),
            pltpu.VMEM((3, width, ny + 2 * PAD, nz), F32),
            pltpu.VMEM((3, width, ny, nz), F32),
            pltpu.VMEM((3, width, ny, nz), F32),
            pltpu.VMEM((STEPS, 2, ny, nz), F32),
            pltpu.VMEM((STEPS, 3, ny + PAD, nz), F32),
            pltpu.VMEM((2, ny, nz), F32),
            padded,
            padded,
            wide,
            wide,
            pltpu.SemaphoreType.DMA((8,)),
            pltpu.SemaphoreType.DMA((2,)),
            pltpu.SemaphoreType.DMA((STEPS,)),
            pltpu.SemaphoreType.DMA((STEPS,)),
            pltpu.SemaphoreType.DMA((2,)),
            pltpu.SemaphoreType.DMA((8,)),
        ],
        compiler_params=params(collective_id=0, has_side_effects=True),
        name="fields",
    )(
        codes,
        sigma_table[None, :],
        eps_table[None, :],
        density_table[None, :],
        tissue,
        e_field,
        h_field,
        phasor_re,
        phasor_im,
    )


def solution(mesh):
    block = P(None, ("parts", "slab"), None, None)
    layers = P(("parts", "slab"), None, None)
    slots = P(("parts", "slab"))
    return jax.shard_map(
        body,
        mesh=mesh,
        in_specs=(
            block,
            block,
            block,
            block,
            layers,
            P(),
            P(),
            P(),
            P(None, ("parts", "slab")),
            slots,
            slots,
        ),
        out_specs=(block, block, P(("parts", "slab"), None)),
        check_vma=False,
    )
```
